32 devices in a mesh: blk: 4 (over y, x), grp: 8 (over z, core).
Axes of the slice: x: 2, y: 2, z: 4, core: 2. Of those that a mesh axis runs over, the one named last changes fastest.
Arguments:
- record: bfloat16 [16448, 8192], P(None, ('blk', 'grp')), may hold values from -400 to 400
- owner_order: int32 [4, 4], replicated, may hold values from 0 to 7, as said below
Outputs:
- cross_spectra: bfloat16 [4, 2, 16, 8192, 256], P(None, None, None, ('blk', 'grp'))
The draws below stay inside these ranges and needn't reach their ends.
Inputs may be any that keep to these rules, and one draw needn't show every extreme that they name: `owner_order`: a channel block position within a group.
All inputs are finite; a program needn't handle non-finite values.
Results may differ from the reference program's by a relative error of at most 0.0071.
Values may be sent and summed in bfloat16 or wider, within the bound.
No kernel may reach another device: no remote copies, remote signals or barrier semaphores. Data moves between devices by JAX's collectives and lax.ppermute only.
A program may use at most 192 MiB of HBM per device.

```python
import math
import jax
import jax.numpy as jnp
from jax import lax

CH = 256
WIN = 256
NS = 128
NB = 16
BIN_LO = 8
ROUNDS = 4
HOP = 64
SAMPLES = 16448
GROUPS = 4
GROUP_BLOCKS = 8
CHANNELS = 8192
N_BLK = 4
N_GRP = 8


def draw_record(key, part):
    keys = jax.random.split(key, 3)
    chan_scale = jnp.exp(jax.random.uniform(keys[0], (CHANNELS,), jnp.float32, 0.0, math.log(10.0)))
    time_scale = jnp.exp(jax.random.uniform(keys[1], (WIN + 1,), jnp.float32, 0.0, math.log(10.0)))
    time_scale = jnp.repeat(time_scale, HOP)
    base = jnp.clip(jax.random.normal(keys[2], (SAMPLES, CHANNELS), jnp.float32), -4.0, 4.0)
    return (base * time_scale[:, None] * chan_scale[None, :]).astype(jnp.bfloat16)


def draw_owner_order(key, part):
    raw = jax.random.randint(key, (ROUNDS, GROUPS), 0, GROUP_BLOCKS, dtype=jnp.int32)
    chosen = jax.random.randint(jax.random.fold_in(key, 1), (), 0, GROUPS, dtype=jnp.int32)
    rows = jnp.arange(ROUNDS, dtype=jnp.int32)[:, None]
    cols = jnp.arange(GROUPS, dtype=jnp.int32)[None, :]
    raw = jnp.where((rows == 0) & (cols == chosen), GROUP_BLOCKS - 1, raw)
    raw = jnp.where((rows == 1) & (cols == chosen), 0, raw)
    return raw.astype(jnp.int32)


def setup_inputs(seed: int = 0) -> dict:
    key_of = jax.random.split(jax.random.key(seed), 3)
    return {
        "record": draw_record(jax.random.fold_in(key_of[2], 71), 0),
        "owner_order": draw_owner_order(jax.random.fold_in(key_of[2], 71), 0),
    }


def band_table():
    sample_index = jnp.arange(NS, dtype=jnp.int32)
    bin_index = BIN_LO + jnp.arange(NB, dtype=jnp.int32)
    phase_int = bin_index[:, None] * sample_index[None, :] % NS
    phase = phase_int.astype(jnp.float32) * (2.0 * math.pi / NS)
    taper = 0.5 - 0.5 * jnp.cos(sample_index.astype(jnp.float32) * (2.0 * math.pi / NS))
    scale = 1.0 / math.sqrt(3.0 * NS / 8.0)
    real_rows = taper[None, :] * jnp.cos(phase) * scale
    imag_rows = -taper[None, :] * jnp.sin(phase) * scale
    return jnp.concatenate([real_rows, imag_rows], axis=0).astype(jnp.bfloat16)

def block_spectra(samples, table):
    halves = samples.reshape(WIN + 1, HOP, samples.shape[1]).astype(jnp.float32)
    table_wide = table.astype(jnp.float32)
    first_half = jnp.einsum('kn,hnc->hkc', table_wide[:, :HOP], halves)
    second_half = jnp.einsum('kn,hnc->hkc', table_wide[:, HOP:], halves)
    half_energy = lax.optimization_barrier(jnp.sum(halves * halves, axis=1))
    window_rms = jnp.sqrt((half_energy[:-1] + half_energy[1:]) / NS + 1e-05)
    raw = first_half[:-1] + second_half[1:]
    return (raw / window_rms[:, None, :]).astype(jnp.bfloat16)

def cross_stack(own, other):
    own_wide = own.astype(jnp.float32)
    other_wide = other.astype(jnp.float32)
    real_own, imag_own = (own_wide[:, :NB], own_wide[:, NB:])
    real_other, imag_other = (other_wide[:, :NB], other_wide[:, NB:])
    real_part = jnp.einsum('wfi,wfj->fij', real_own, real_other) + jnp.einsum('wfi,wfj->fij', imag_own, imag_other)
    imag_part = jnp.einsum('wfi,wfj->fij', imag_own, real_other) - jnp.einsum('wfi,wfj->fij', real_own, imag_other)
    return jnp.stack([real_part, imag_part], axis=0) / math.sqrt(WIN)

def reference(record, owner_order):
    table = band_table()
    blocks = N_BLK * N_GRP

    def one_block(index):
        samples = lax.dynamic_slice_in_dim(record, (index * CH).astype(jnp.int32), CH, 1)
        return block_spectra(samples, table)
    all_spectra = lax.map(one_block, jnp.arange(blocks, dtype=jnp.int32))

    def one_pair_set(index):
        my_group = index // N_GRP
        results = []
        for round_index in range(ROUNDS):
            partner = (my_group - round_index) % N_BLK * N_GRP + owner_order[round_index, my_group]
            results.append(cross_stack(all_spectra[index], all_spectra[partner.astype(jnp.int32)]))
        return jnp.stack(results, axis=0).astype(jnp.bfloat16)
    stacked = lax.map(one_pair_set, jnp.arange(blocks, dtype=jnp.int32))
    stacked = jnp.transpose(stacked, (1, 2, 3, 0, 4, 5))
    return stacked.reshape(ROUNDS, 2, NB, blocks * CH, CH)
```

```python
import functools
import math

import jax
import jax.numpy as jnp
import numpy as np
from jax import lax
from jax.experimental import pallas as pl
from jax.experimental.pallas import tpu as pltpu
from jax.sharding import PartitionSpec as P

WIN = 256
NS = 128
NB = 16
BIN_LO = 8
ROUNDS = 4
HOP = 64
WG = 16
CORES = 2
HALF = NB // CORES
FIRST = 2
LAG = 2
ORDER = (1, 3, 2, 0)
HBM = pltpu.MemorySpace.HBM


def band_table():
    n = np.arange(NS)
    q = BIN_LO + np.arange(NB)
    phase = ((q[:, None] * n[None, :]) % NS) * (2.0 * math.pi / NS)
    taper = 0.5 - 0.5 * np.cos(n * (2.0 * math.pi / NS))
    scale = 1.0 / math.sqrt(3.0 * NS / 8.0)
    real = taper * np.cos(phase) * scale
    imag = -taper * np.sin(phase) * scale
    return np.stack([real, imag], axis=1).astype(np.float32)


def banded(bins):
    table = band_table()[bins]
    out = np.zeros((len(bins), 2, WG, (WG + 1) * HOP), np.float32)
    for w in range(WG):
        out[:, :, w, w * HOP : w * HOP + NS] = table
    return out.reshape(len(bins) * 2 * WG, (WG + 1) * HOP)


def tables(lo, hi):
    both = [banded(np.arange(h * HALF + lo, h * HALF + hi)) for h in range(CORES)]
    return jnp.asarray(np.stack(both).astype(jnp.bfloat16))


def half_energy(x):
    wide = x.astype(jnp.float32)
    return jnp.sum((wide * wide).reshape(-1, HOP, x.shape[-1]), axis=1)


def band_kernel(first, core_ref, main_ref, halo_ref, mine_table, other_table, *refs):
    main, halo = main_ref[...], halo_ref[...]
    if first:
        mine_ref, other_ref, inv_ref = refs
        energy = half_energy(main)
        later = jnp.concatenate([energy[1:], half_energy(halo)], axis=0)
        inv = 1.0 / jnp.sqrt((energy + later) / NS + 1e-05)
        inv_ref[...] = inv
    else:
        inv_ref, mine_ref, other_ref = refs
        inv = inv_ref[...]
    split = WG * HOP
    for table, out in ((mine_table, mine_ref), (other_table, other_ref)):
        raw = jnp.dot(table[0, :, :split], main, preferred_element_type=jnp.float32)
        raw += jnp.dot(table[0, :, split:], halo, preferred_element_type=jnp.float32)
        raw = raw.reshape(-1, 2, WG, main.shape[1])
        out[...] = (raw * inv).astype(jnp.bfloat16)


def band(record, core, lo, hi, inv=None):
    channels = record.shape[1]
    table = tables(lo, hi)
    rows = table.shape[1]
    first = inv is None
    spectra_spec = pl.BlockSpec((hi - lo, 2, WG, channels), lambda i, c: (0, 0, i, 0))
    inv_spec = pl.BlockSpec((WG, channels), lambda i, c: (i, 0))
    spectra = jax.ShapeDtypeStruct((hi - lo, 2, WIN, channels), jnp.bfloat16)
    in_specs = [
        pl.BlockSpec((WG * HOP, channels), lambda i, c: (i, 0)),
        pl.BlockSpec((HOP, channels), lambda i, c: ((i + 1) * WG, 0)),
        pl.BlockSpec((1, rows, table.shape[2]), lambda i, c: (c[0], 0, 0)),
        pl.BlockSpec((1, rows, table.shape[2]), lambda i, c: (1 - c[0], 0, 0)),
    ]
    out_specs, out_shape = [spectra_spec] * 2, [spectra] * 2
    args = [core, record, record, table, table]
    if first:
        out_specs.append(inv_spec)
        out_shape.append(jax.ShapeDtypeStruct((WIN, channels), jnp.float32))
    else:
        in_specs.append(inv_spec)
        args.append(inv)
    return pl.pallas_call(
        functools.partial(band_kernel, first),
        grid_spec=pltpu.PrefetchScalarGridSpec(
            num_scalar_prefetch=1,
            grid=(WIN // WG,),
            in_specs=in_specs,
            out_specs=out_specs,
        ),
        out_shape=out_shape,
        name="band_first" if first else "band_rest",
        compiler_params=pltpu.CompilerParams(vmem_limit_bytes=48 * 2**20),
        cost_estimate=pl.CostEstimate(
            flops=4 * rows * WIN // WG * table.shape[2] * channels,
            bytes_accessed=2 * record.size,
            transcendentals=0,
        ),
    )(*args)


def route(plan, moves):
    arrays = []

    def place(a):
        for i, b in enumerate(arrays):
            if b is a:
                return i
        arrays.append(a)
        return len(arrays) - 1

    laid = []
    for step, column, pieces, singles in moves:
        laid.append((step, column, [[place(a) for a in group] for group in pieces], [place(a) for a in singles]))
    shape = moves[0][2][0][0].shape[1:]

    def kernel(plan_ref, *refs):
        ins, outs, sems = refs[: len(arrays)], refs[len(arrays) : -1], refs[-1]
        for m, (step, column, pieces, singles) in enumerate(laid):
            which, row = plan_ref[step, column], plan_ref[step, column + 1]
            for g, group in enumerate(pieces):
                base = 0
                for a in group:
                    count = ins[a].shape[0]

                    @pl.when((which == g) & (row >= base) & (row < base + count))
                    def _(a=a, base=base, m=m, row=row, count=count):
                        index = jnp.clip(row - base, 0, count - 1)
                        pltpu.make_async_copy(ins[a].at[index], outs[m], sems.at[m]).start()

                    base += count
            for g, a in enumerate(singles):

                @pl.when(which == len(pieces) + g)
                def _(a=a, m=m):
                    pltpu.make_async_copy(ins[a], outs[m], sems.at[m]).start()

        for m in range(len(laid)):
            pltpu.make_async_copy(outs[m], outs[m], sems.at[m]).wait()

    size = math.prod(shape)
    return pl.pallas_call(
        kernel,
        in_specs=[pl.BlockSpec(memory_space=pltpu.SMEM)] + [pl.BlockSpec(memory_space=HBM)] * len(arrays),
        out_specs=[pl.BlockSpec(memory_space=HBM)] * len(laid),
        out_shape=[jax.ShapeDtypeStruct(shape, jnp.bfloat16)] * len(laid),
        scratch_shapes=[pltpu.SemaphoreType.DMA((len(laid),))],
        name="route",
        cost_estimate=pl.CostEstimate(flops=0, bytes_accessed=4 * size * len(laid), transcendentals=0),
    )(plan, *arrays)


def transposed_dot(a, b):
    return lax.dot_general(a, b, (((0,), (0,)), ((), ())), preferred_element_type=jnp.float32)


def cross_kernel(core_ref, mine_ref, other_ref, near_ref, far_ref, *refs):
    out_ref = refs[-1]

    def emit(own, paired):
        p, q, pj, qj = own[0, 0], own[0, 1], paired[0], paired[1]
        scale = 1.0 / math.sqrt(WIN)
        real = transposed_dot(p, pj) + transposed_dot(q, qj)
        imag = transposed_dot(q, pj) - transposed_dot(p, qj)
        out_ref[0, 0, 0] = (real * scale).astype(jnp.bfloat16)
        out_ref[0, 1, 0] = (imag * scale).astype(jnp.bfloat16)

    @pl.when(pl.program_id(0) == 0)
    def _():
        emit(mine_ref, near_ref)

    @pl.when(pl.program_id(0) == 1)
    def _():
        emit(other_ref, far_ref)


def cross(out, core, mine, other, row, near, far, round_index, bin_index):
    channels = near.shape[-1]
    own_spec = pl.BlockSpec((1, 2, WIN, channels), lambda g, c: (row, 0, 0, 0))
    paired_spec = pl.BlockSpec((2, WIN, channels), lambda g, c: (0, 0, 0))
    out_spec = pl.BlockSpec(
        (1, 2, 1, channels, channels),
        lambda g, c: (round_index, 0, ((c[0] + g) % CORES) * HALF + bin_index, 0, 0),
    )
    in_specs = [own_spec, own_spec, paired_spec, paired_spec]
    args = [core, mine, other, near, far]
    aliases = {}
    if out is not None:
        in_specs.append(pl.BlockSpec(memory_space=HBM))
        args.append(out)
        aliases = {len(args) - 1: 0}
    return pl.pallas_call(
        cross_kernel,
        grid_spec=pltpu.PrefetchScalarGridSpec(
            num_scalar_prefetch=1, grid=(CORES,), in_specs=in_specs, out_specs=out_spec
        ),
        out_shape=jax.ShapeDtypeStruct((ROUNDS, 2, NB, channels, channels), jnp.bfloat16),
        input_output_aliases=aliases,
        name="cross",
        compiler_params=pltpu.CompilerParams(vmem_limit_bytes=32 * 2**20),
        cost_estimate=pl.CostEstimate(
            flops=16 * WIN * channels * channels,
            bytes_accessed=12 * WIN * channels * 2,
            transcendentals=0,
        ),
    )(*args)


def body(record, owner_order):
    groups, members = lax.axis_size("blk"), lax.axis_size("grp")
    chips = members // CORES
    group, member = lax.axis_index("blk"), lax.axis_index("grp")
    chip, core = member // CORES, member % CORES
    core_arg = core.reshape(1).astype(jnp.int32)

    up = [(m, m + CORES) for m in range(members - CORES)]
    down = [(m + CORES, m) for m in range(members - CORES)]
    swap = [(m, m ^ 1) for m in range(members)]

    order = np.array(ORDER)
    asked = jnp.stack([owner_order[r, (group + r) % groups] for r in ORDER])
    chunks = ROUNDS * HALF
    steps = chunks + LAG * (chips - 2)
    links = chips - 1

    def source_of(k):
        k = jnp.clip(k, 0, chunks - 1)
        owner = jnp.take(asked, k // HALF)
        return owner // CORES, (owner % CORES != core).astype(jnp.int32), k % HALF

    t = jnp.arange(steps, dtype=jnp.int32)
    columns = []
    for hop in (chip, chips - 1 - chip):
        home, held, row = source_of(t - LAG * hop)
        columns += [jnp.where((home == chip) | (t < LAG), held, 2), row]
    home, held, row = source_of(t)
    arrived = jnp.where(home < chip, 2 + chip - 1, 2 + links + chips - 2 - chip)
    columns += [jnp.where(home == chip, held, arrived), row]
    plan = jnp.stack(columns, axis=1).astype(jnp.int32)

    mine_a, other_a, inv = band(record, core_arg, 0, FIRST)
    twin_a = lax.ppermute(other_a, "grp", swap)
    mine_b, other_b = band(record, core_arg, FIRST, HALF, inv)
    twin_b = lax.ppermute(other_b, "grp", swap)

    from_below, from_above = [], []
    out = None
    for step in range(steps + 1):
        if step < FIRST:
            held = [[mine_a], [twin_a]]
        else:
            held = [[mine_a, mine_b], [twin_a, twin_b]]
        moves = []
        if step < steps:
            below = [from_below[step - LAG]] if step >= LAG else []
            above = [from_above[step - LAG]] if step >= LAG else []
            moves += [(step, 0, held, below), (step, 2, held, above)]
        k = step - LAG * (chips - 2) - 1
        if k >= 0:
            candidates = [from_below[k + LAG * j] for j in range(links)]
            candidates += [from_above[k + LAG * j] for j in range(links)]
            moves.append((k, 4, held, candidates))
        sent = route(plan, moves)
        if step < steps:
            from_below.append(lax.ppermute(sent[0], "grp", up))
            from_above.append(lax.ppermute(sent[1], "grp", down))
        if k >= 0:
            round_index, bin_index = ORDER[k // HALF], k % HALF
            near = sent[-1]
            if round_index:
                pairs = [(g, (g + round_index) % groups) for g in range(groups)]
                near = lax.ppermute(near, "blk", pairs)
            far = lax.ppermute(near, "grp", swap)
            own = (mine_a, other_a, bin_index) if bin_index < FIRST else (mine_b, other_b, bin_index - FIRST)
            out = cross(out, core_arg, *own, near, far, round_index, bin_index)
    return out


def solution(mesh):
    return jax.shard_map(
        body,
        mesh=mesh,
        in_specs=(P(None, ("blk", "grp")), P()),
        out_specs=P(None, None, None, ("blk", "grp"), None),
        check_vma=False,
    )
```

```python
import functools
import math

import jax
import jax.numpy as jnp
import numpy as np
from jax import lax
from jax.experimental import pallas as pl
from jax.experimental.pallas import tpu as pltpu
from jax.sharding import PartitionSpec as P

WIN = 256
NS = 128
NB = 16
BIN_LO = 8
ROUNDS = 4
HOP = 64
WG = 16
CORES = 2
HALF = NB // CORES
FIRST = 4
GROUP = 4
GAP = 5
REST_AT = 1
LAG = 2
ORDER = ((1, 0), (2, 0), (3, 0), (1, 1), (2, 1), (3, 1), (0, 0), (0, 1))
VMEM = 8 * 2**20
SHORT = pl.CostEstimate(flops=1, bytes_accessed=1, transcendentals=0)


def band_table():
    n = np.arange(NS)
    q = BIN_LO + np.arange(NB)
    phase = ((q[:, None] * n[None, :]) % NS) * (2.0 * math.pi / NS)
    taper = 0.5 - 0.5 * np.cos(n * (2.0 * math.pi / NS))
    scale = 1.0 / math.sqrt(3.0 * NS / 8.0)
    real = taper * np.cos(phase) * scale
    imag = -taper * np.sin(phase) * scale
    return np.stack([real, imag], axis=1).astype(np.float32)


def banded(lo, hi):
    table = band_table().reshape(CORES, HALF, 2, NS)[:, lo:hi].swapaxes(0, 1)
    out = np.zeros((hi - lo, CORES, 2, WG, (WG + 1) * HOP), np.float32)
    for w in range(WG):
        out[..., w, w * HOP : w * HOP + NS] = table
    return jnp.asarray(out.reshape(-1, (WG + 1) * HOP).astype(jnp.bfloat16))


def in_hbm():
    return pl.BlockSpec(memory_space=pltpu.MemorySpace.HBM)


def token_shape():
    return jax.ShapeDtypeStruct((8, 128), jnp.int32)


def in_place():
    return pl.BlockSpec(memory_space=pl.ANY)


def half_energy(x):
    wide = x.astype(jnp.float32)
    return jnp.sum((wide * wide).reshape(-1, HOP, x.shape[-1]), axis=1)


def band_kernel(first, core_ref, main_ref, halo_ref, table, *refs):
    main, halo = main_ref[...], halo_ref[...]
    if first:
        out, inv_ref, _ = refs
        energy = half_energy(main)
        later = jnp.concatenate([energy[1:], half_energy(halo)], axis=0)
        inv = 1.0 / jnp.sqrt((energy + later) / NS + 1e-05)
        inv_ref[...] = inv
    else:
        inv_ref, _, out, _ = refs
        inv = inv_ref[...]
    split = WG * HOP
    raw = jnp.dot(table[:, :split], main, preferred_element_type=jnp.float32)
    raw += jnp.dot(table[:, split:], halo, preferred_element_type=jnp.float32)
    raw = raw.reshape(-1, CORES, 2, WG, main.shape[1])
    out[...] = (raw * inv).astype(jnp.bfloat16)


def band(core, record, lo, hi, inv=None, token=None):
    channels = record.shape[1]
    table = banded(lo, hi)
    rows = table.shape[0]
    first = inv is None
    inv_spec = pl.BlockSpec((WG, channels), lambda i: (i, 0))
    in_specs = [
        pl.BlockSpec(memory_space=pltpu.SMEM),
        pl.BlockSpec((WG * HOP, channels), lambda i: (i, 0)),
        pl.BlockSpec((HOP, channels), lambda i: ((i + 1) * WG, 0)),
        pl.BlockSpec(table.shape, lambda i: (0, 0)),
    ]
    out_specs = [pl.BlockSpec((hi - lo, CORES, 2, WG, channels), lambda i: (0, 0, 0, i, 0))]
    out_shape = [jax.ShapeDtypeStruct((hi - lo, CORES, 2, WIN, channels), jnp.bfloat16)]
    args = [core, record, record, table]
    if first:
        out_specs.append(inv_spec)
        out_shape.append(jax.ShapeDtypeStruct((WIN, channels), jnp.float32))
    else:
        in_specs += [inv_spec, in_place()]
        args += [inv, token]
    return pl.pallas_call(
        functools.partial(band_kernel, first),
        grid=(WIN // WG,),
        in_specs=in_specs,
        out_specs=out_specs + [in_place()],
        out_shape=out_shape + [token_shape()],
        name="band_first" if first else "band_rest",
        compiler_params=pltpu.CompilerParams(vmem_limit_bytes=VMEM),
        cost_estimate=pl.CostEstimate(
            flops=2 * rows * (WIN // WG) * table.shape[1] * channels, bytes_accessed=3 * record.size, transcendentals=0
        ),
    )(*args)


def turn_kernel(in_ref, _, out_ref, __):
    for part in range(2):
        out_ref[0, 0, :, part * WIN : (part + 1) * WIN] = in_ref[0, 0, part].T


def turn(spectra, token):
    count, channels = spectra.shape[0], spectra.shape[-1]
    return pl.pallas_call(
        turn_kernel,
        grid=(count, CORES),
        in_specs=[pl.BlockSpec((1, 1, 2, WIN, channels), lambda i, h: (i, h, 0, 0, 0)), in_place()],
        out_specs=[pl.BlockSpec((1, 1, channels, 2 * WIN), lambda i, h: (i, h, 0, 0)), in_place()],
        out_shape=[jax.ShapeDtypeStruct((count, CORES, channels, 2 * WIN), jnp.bfloat16), token_shape()],
        name="turn",
        compiler_params=pltpu.CompilerParams(vmem_limit_bytes=VMEM),
        cost_estimate=SHORT,
    )(spectra, token)


def place(arrays, a):
    for i, b in enumerate(arrays):
        if b is a:
            return i
    arrays.append(a)
    return len(arrays) - 1


def seat():
    member = lax.axis_index("grp")
    return lax.axis_index("blk"), member // CORES, member % CORES, lax.axis_size("grp") // CORES


def chunk_of(k):
    r, half = ORDER[k // GROUP]
    return r, half * GROUP + k % GROUP


def asked_of(orders, k):
    r, _ = chunk_of(k)
    return orders[r, lax.rem(lax.axis_index("blk") + r, lax.axis_size("blk"))]


def inject(orders, token, step, mine, twin, held):
    chips = lax.axis_size("grp") // CORES
    sent = [step - LAG * hop for hop in range(chips)]
    hops = [hop for hop in range(chips) if 0 <= sent[hop] < ROUNDS * HALF]
    arrays, slots = [], {}
    for hop in hops:
        _, row = chunk_of(sent[hop])
        slots[hop] = (place(arrays, mine[row // FIRST]), row % FIRST), (place(arrays, twin[row]), None)
    whole = twin[0].shape

    def kernel(orders_ref, *refs):
        ins, out, buffer, sem = refs[: len(arrays)], refs[-4], refs[-2], refs[-1]
        _, chip, core, _ = seat()
        seen = jnp.where(core == 0, chip, chips - 1 - chip)
        for hop in hops:
            owner = asked_of(orders_ref, sent[hop])
            here = (seen == hop) & (owner // CORES == chip)
            for (slot, row), same in zip(slots[hop], (True, False), strict=True):
                source = ins[slot] if row is None else ins[slot].at[row]

                @pl.when(here & ((owner % CORES == core) == same))
                def _(source=source):
                    load = pltpu.make_async_copy(source, buffer, sem.at[0])
                    load.start()
                    load.wait()
                    store = pltpu.make_async_copy(buffer, out, sem.at[1])
                    store.start()
                    store.wait()

    in_specs = [pl.BlockSpec(memory_space=pltpu.SMEM)] + [in_hbm()] * len(arrays) + [in_place()]
    args = [orders, *arrays, token]
    aliases = {}
    if held is not None:
        in_specs.append(in_place())
        args.append(held)
        aliases = {len(args) - 1: 0}
    return pl.pallas_call(
        kernel,
        in_specs=in_specs,
        out_specs=[in_place()] * 2,
        out_shape=[jax.ShapeDtypeStruct(whole, jnp.bfloat16), token_shape()],
        input_output_aliases=aliases,
        scratch_shapes=[pltpu.VMEM(whole, jnp.bfloat16), pltpu.SemaphoreType.DMA((2,))],
        name="inject",
        compiler_params=pltpu.CompilerParams(vmem_limit_bytes=4 * 2**20),
        cost_estimate=SHORT,
    )(*args)


def gather(orders, token, ks, held, swapped=None):
    arrays = []
    chips = lax.axis_size("grp") // CORES
    slots = {(k, j): place(arrays, held[k + LAG * j]) for k in ks for j in range(chips - 1)}
    extra = [] if swapped is None else [swapped]
    shape = held[0].shape[1:]

    def kernel(orders_ref, *refs):
        ins, out, sems = refs[: len(arrays)], refs[-3], refs[-1]
        _, chip, core, _ = seat()
        hop = jnp.where(core == 0, chip, chips - 1 - chip)
        home = asked_of(orders_ref, ks[0]) // CORES
        has = (hop >= 1) & ((home == chip) | ((core == 0) == (home < chip)))
        half = 1 - core if swapped is None else core
        lead = jnp.maximum(hop, 1) - 1
        for j in range(chips - 1):

            @pl.when((lead == j) & (has if swapped is not None else lead == j))
            def _(j=j):
                for m, k in enumerate(ks):
                    pltpu.make_async_copy(ins[slots[k, j]].at[half], out.at[m], sems.at[m]).start()

        if swapped is not None:

            @pl.when(jnp.logical_not(has))
            def _():
                for m in range(len(ks)):
                    pltpu.make_async_copy(refs[len(arrays)].at[m], out.at[m], sems.at[m]).start()

        for m in range(len(ks)):
            pltpu.make_async_copy(out.at[m], out.at[m], sems.at[m]).wait()

    return pl.pallas_call(
        kernel,
        in_specs=[pl.BlockSpec(memory_space=pltpu.SMEM)] + [in_place()] * (len(arrays) + len(extra) + 1),
        out_specs=[pl.BlockSpec(memory_space=pltpu.VMEM), in_place()],
        out_shape=[jax.ShapeDtypeStruct((len(ks), *shape), jnp.bfloat16), token_shape()],
        scratch_shapes=[pltpu.SemaphoreType.DMA((len(ks),))],
        name="collect" if swapped is None else "select",
        compiler_params=pltpu.CompilerParams(vmem_limit_bytes=8 * 2**20),
        cost_estimate=SHORT,
    )(orders, *arrays, *extra, token)


def cross_kernel(core_ref, own_ref, near_ref, far_ref, *refs):
    out_ref = refs[-2]

    def emit(paired_ref):
        own = own_ref[0, 0]
        turned = jnp.concatenate([own[:, WIN:], -own[:, :WIN]], axis=1)
        paired = paired_ref[0].reshape(2 * WIN, -1)
        scale = 1.0 / math.sqrt(WIN)
        for part, lhs in enumerate((own, turned)):
            total = jnp.dot(lhs, paired, preferred_element_type=jnp.float32)
            out_ref[0, part, 0] = (total * scale).astype(jnp.bfloat16)

    @pl.when(pl.program_id(1) == 0)
    def _():
        emit(near_ref)

    @pl.when(pl.program_id(1) == 1)
    def _():
        emit(far_ref)


def cross(out, token, core, own, near, far, round_index, first_chunk, begin, count):
    channels = near.shape[-1]
    first_chunk += begin
    row = first_chunk % own.shape[0]
    paired_spec = pl.BlockSpec((1, 2, WIN, channels), lambda i, g, c: (begin + i, 0, 0, 0))
    in_specs = [
        pl.BlockSpec((1, 1, channels, 2 * WIN), lambda i, g, c: (row + i, (c[0] + g) % CORES, 0, 0)),
        paired_spec,
        paired_spec,
        in_place(),
    ]
    out_spec = pl.BlockSpec(
        (1, 2, 1, channels, channels),
        lambda i, g, c: (round_index, 0, ((c[0] + g) % CORES) * HALF + first_chunk + i, 0, 0),
    )
    args = [core, own, near, far, token]
    aliases = {}
    if out is not None:
        in_specs.append(in_place())
        args.append(out)
        aliases = {len(args) - 1: 0}
    return pl.pallas_call(
        cross_kernel,
        grid_spec=pltpu.PrefetchScalarGridSpec(
            num_scalar_prefetch=1, grid=(count, CORES), in_specs=in_specs, out_specs=[out_spec, in_place()]
        ),
        out_shape=[jax.ShapeDtypeStruct((ROUNDS, 2, NB, channels, channels), jnp.bfloat16), token_shape()],
        input_output_aliases=aliases,
        name="cross",
        compiler_params=pltpu.CompilerParams(vmem_limit_bytes=VMEM),
        cost_estimate=SHORT,
    )(*args)


def body(record, owner_order):
    groups, members = lax.axis_size("blk"), lax.axis_size("grp")
    chips = members // CORES
    core_arg = (lax.axis_index("grp") % CORES).reshape(1).astype(jnp.int32)

    flow = [(m, m + CORES) for m in range(0, members - CORES, CORES)]
    flow += [(m + CORES, m) for m in range(1, members - CORES, CORES)]
    swap = [(m, m ^ 1) for m in range(members)]
    chunks = ROUNDS * HALF
    steps = chunks + LAG * (chips - 2)

    mine_a, inv, token = band(core_arg, record, 0, FIRST)
    mine, twin = [mine_a], [lax.ppermute(mine_a[i], "grp", swap) for i in range(FIRST)]

    arrived, held, turned = [], [], []
    out = None
    kept, nears, fars = {}, {}, {}
    todo = {}
    for g in range(chunks // GROUP):
        at = (g + 1) * GROUP - 1 + LAG * (chips - 2) + LAG
        across = bool(ORDER[g][0])
        left = chunks // GROUP - 1 - g
        pick = at + (1, 3, 3)[left] if left < 3 else at + GAP
        give = pick + 5 if across else pick
        meet = (pick + 1, pick + 3, give + 1)[left] if left < 3 else give + GAP
        plan = ((at, "collect", 0), (pick, "select", 0), (give, "pass_over", 0), (meet, "cross", 0), (meet + (left >= 3), "cross", 1))
        for wait, what, part in plan:
            todo.setdefault(wait, []).append((what, g, part))

    for step in range(max(todo) + 1):
        if step < steps + LAG:
            buffer = arrived[step - LAG] if step >= LAG else None
            sent, token = inject(owner_order, token, step, mine, twin, buffer)
            if step < steps:
                arrived.append(lax.ppermute(sent, "grp", flow))
            if step >= LAG:
                held.append(sent)
        if step == REST_AT:
            mine_b, token = band(core_arg, record, FIRST, HALF, inv, token)
            mine.append(mine_b)
            twin += [lax.ppermute(mine_b[i], "grp", swap) for i in range(HALF - FIRST)]
        if step in (5, 7):
            part, token = turn(mine[0] if step == 5 else mine[1], token)
            turned.append(part)
        for what, g, part in todo.get(step, ()):
            first = g * GROUP
            ks = range(first, first + GROUP)
            r, begin = chunk_of(first)
            if what == "collect":
                given, token = gather(owner_order, token, ks, held)
                kept[g] = lax.ppermute(given, "grp", swap)
            elif what == "select":
                near, token = gather(owner_order, token, ks, held, kept[g])
                if r:
                    near = lax.ppermute(near, "blk", [(b, (b + r) % groups) for b in range(groups)])
                nears[g] = near
            elif what == "pass_over":
                fars[g] = lax.ppermute(nears[g], "grp", swap)
            else:
                own, count = turned[begin // FIRST], GROUP // 2
                out, token = cross(out, token, core_arg, own, nears[g], fars[g], r, begin, part * count, count)
    return out


def solution(mesh):
    return jax.shard_map(
        body,
        mesh=mesh,
        in_specs=(P(None, ("blk", "grp")), P()),
        out_specs=P(None, None, None, ("blk", "grp"), None),
        check_vma=False,
    )
```

```python
import functools
import math

import jax
import jax.numpy as jnp
import numpy as np
from jax import lax
from jax.experimental import pallas as pl
from jax.experimental.pallas import tpu as pltpu
from jax.sharding import PartitionSpec as P

WIN = 256
NS = 128
NB = 16
BIN_LO = 8
ROUNDS = 4
HOP = 64
WG = 16
CORES = 2
HALF = NB // CORES
FIRST = 4
GROUP = 4
PICK = 3
GIVE = 5
TAIL = (2, 5, 9, 11)
PARTS, TURN = 2, (5, 7)
GAP = 5
REST_AT = 1
LAG = 2
ORDER = ((1, 0), (1, 1), (3, 0), (3, 1), (2, 0), (2, 1), (0, 0), (0, 1))
VMEM = 8 * 2**20
SHORT = pl.CostEstimate(flops=1, bytes_accessed=1, transcendentals=0)


def band_table():
    n = np.arange(NS)
    q = BIN_LO + np.arange(NB)
    phase = ((q[:, None] * n[None, :]) % NS) * (2.0 * math.pi / NS)
    taper = 0.5 - 0.5 * np.cos(n * (2.0 * math.pi / NS))
    scale = 1.0 / math.sqrt(3.0 * NS / 8.0)
    real = taper * np.cos(phase) * scale
    imag = -taper * np.sin(phase) * scale
    return np.stack([real, imag], axis=1).astype(np.float32)


def banded(lo, hi):
    table = band_table().reshape(CORES, HALF, 2, NS)[:, lo:hi].swapaxes(0, 1)
    out = np.zeros((hi - lo, CORES, 2, WG, (WG + 1) * HOP), np.float32)
    for w in range(WG):
        out[..., w, w * HOP : w * HOP + NS] = table
    return jnp.asarray(out.reshape(-1, (WG + 1) * HOP).astype(jnp.bfloat16))


def in_hbm():
    return pl.BlockSpec(memory_space=pltpu.MemorySpace.HBM)


def token_shape():
    return jax.ShapeDtypeStruct((8, 128), jnp.int32)


def in_place():
    return pl.BlockSpec(memory_space=pl.ANY)


def half_energy(x):
    wide = x.astype(jnp.float32)
    return jnp.sum((wide * wide).reshape(-1, HOP, x.shape[-1]), axis=1)


def band_kernel(first, core_ref, main_ref, halo_ref, table, *refs):
    main, halo = main_ref[...], halo_ref[...]
    if first:
        out, inv_ref, _ = refs
        energy = half_energy(main)
        later = jnp.concatenate([energy[1:], half_energy(halo)], axis=0)
        inv = 1.0 / jnp.sqrt((energy + later) / NS + 1e-05)
        inv_ref[...] = inv
    else:
        inv_ref, _, out, _ = refs
        inv = inv_ref[...]
    split = WG * HOP
    raw = jnp.dot(table[:, :split], main, preferred_element_type=jnp.float32)
    raw += jnp.dot(table[:, split:], halo, preferred_element_type=jnp.float32)
    raw = raw.reshape(-1, CORES, 2, WG, main.shape[1])
    out[...] = (raw * inv).astype(jnp.bfloat16)


def band(core, record, lo, hi, inv=None, token=None):
    channels = record.shape[1]
    table = banded(lo, hi)
    rows = table.shape[0]
    first = inv is None
    inv_spec = pl.BlockSpec((WG, channels), lambda i: (i, 0))
    in_specs = [
        pl.BlockSpec(memory_space=pltpu.SMEM),
        pl.BlockSpec((WG * HOP, channels), lambda i: (i, 0)),
        pl.BlockSpec((HOP, channels), lambda i: ((i + 1) * WG, 0)),
        pl.BlockSpec(table.shape, lambda i: (0, 0)),
    ]
    out_specs = [pl.BlockSpec((hi - lo, CORES, 2, WG, channels), lambda i: (0, 0, 0, i, 0))]
    out_shape = [jax.ShapeDtypeStruct((hi - lo, CORES, 2, WIN, channels), jnp.bfloat16)]
    args = [core, record, record, table]
    if first:
        out_specs.append(inv_spec)
        out_shape.append(jax.ShapeDtypeStruct((WIN, channels), jnp.float32))
    else:
        in_specs += [inv_spec, in_place()]
        args += [inv, token]
    return pl.pallas_call(
        functools.partial(band_kernel, first),
        grid=(WIN // WG,),
        in_specs=in_specs,
        out_specs=out_specs + [in_place()],
        out_shape=out_shape + [token_shape()],
        name="band_first" if first else "band_rest",
        compiler_params=pltpu.CompilerParams(vmem_limit_bytes=VMEM),
        cost_estimate=pl.CostEstimate(
            flops=2 * rows * (WIN // WG) * table.shape[1] * channels, bytes_accessed=3 * record.size, transcendentals=0
        ),
    )(*args)


def turn_kernel(in_ref, _, out_ref, __):
    for part in range(2):
        out_ref[0, 0, :, part * WIN : (part + 1) * WIN] = in_ref[0, 0, part].T


def turn(spectra, token):
    count, channels = spectra.shape[0], spectra.shape[-1]
    return pl.pallas_call(
        turn_kernel,
        grid=(count, CORES),
        in_specs=[pl.BlockSpec((1, 1, 2, WIN, channels), lambda i, h: (i, h, 0, 0, 0)), in_place()],
        out_specs=[pl.BlockSpec((1, 1, channels, 2 * WIN), lambda i, h: (i, h, 0, 0)), in_place()],
        out_shape=[jax.ShapeDtypeStruct((count, CORES, channels, 2 * WIN), jnp.bfloat16), token_shape()],
        name="turn",
        compiler_params=pltpu.CompilerParams(vmem_limit_bytes=VMEM),
        cost_estimate=SHORT,
    )(spectra, token)


def place(arrays, a):
    for i, b in enumerate(arrays):
        if b is a:
            return i
    arrays.append(a)
    return len(arrays) - 1


def seat():
    member = lax.axis_index("grp")
    return lax.axis_index("blk"), member // CORES, member % CORES, lax.axis_size("grp") // CORES


def chunk_of(k):
    r, half = ORDER[k // GROUP]
    return r, half * GROUP + k % GROUP


def asked_of(orders, k):
    r, _ = chunk_of(k)
    return orders[r, lax.rem(lax.axis_index("blk") + r, lax.axis_size("blk"))]


def inject(orders, token, step, mine, twin, held):
    chips = lax.axis_size("grp") // CORES
    sent = [step - LAG * hop for hop in range(chips)]
    hops = [hop for hop in range(chips) if 0 <= sent[hop] < ROUNDS * HALF]
    arrays, slots = [], {}
    for hop in hops:
        _, row = chunk_of(sent[hop])
        slots[hop] = (place(arrays, mine[row // FIRST]), row % FIRST), (place(arrays, twin[row]), None)
    whole = twin[0].shape

    def kernel(orders_ref, *refs):
        ins, out, buffer, sem = refs[: len(arrays)], refs[-4], refs[-2], refs[-1]
        _, chip, core, _ = seat()
        seen = jnp.where(core == 0, chip, chips - 1 - chip)
        for hop in hops:
            owner = asked_of(orders_ref, sent[hop])
            here = (seen == hop) & (owner // CORES == chip)
            for (slot, row), same in zip(slots[hop], (True, False), strict=True):
                source = ins[slot] if row is None else ins[slot].at[row]

                @pl.when(here & ((owner % CORES == core) == same))
                def _(source=source):
                    load = pltpu.make_async_copy(source, buffer, sem.at[0])
                    load.start()
                    load.wait()
                    store = pltpu.make_async_copy(buffer, out, sem.at[1])
                    store.start()
                    store.wait()

    in_specs = [pl.BlockSpec(memory_space=pltpu.SMEM)] + [in_hbm()] * len(arrays) + [in_place()]
    args = [orders, *arrays, token]
    aliases = {}
    if held is not None:
        in_specs.append(in_place())
        args.append(held)
        aliases = {len(args) - 1: 0}
    return pl.pallas_call(
        kernel,
        in_specs=in_specs,
        out_specs=[in_place()] * 2,
        out_shape=[jax.ShapeDtypeStruct(whole, jnp.bfloat16), token_shape()],
        input_output_aliases=aliases,
        scratch_shapes=[pltpu.VMEM(whole, jnp.bfloat16), pltpu.SemaphoreType.DMA((2,))],
        name="inject",
        compiler_params=pltpu.CompilerParams(vmem_limit_bytes=4 * 2**20),
        cost_estimate=SHORT,
    )(*args)


def gather(orders, token, ks, held, swapped=None):
    arrays = []
    chips = lax.axis_size("grp") // CORES
    slots = {(k, j): place(arrays, held[k + LAG * j]) for k in ks for j in range(chips - 1)}
    extra = [] if swapped is None else swapped
    apart = swapped is None
    shape = held[0].shape[1:]

    def kernel(orders_ref, *refs):
        ins, sems = refs[: len(arrays)], refs[-1]
        outs = refs[-2 - len(ks) : -2] if apart else [refs[-3].at[m] for m in range(len(ks))]
        _, chip, core, _ = seat()
        hop = jnp.where(core == 0, chip, chips - 1 - chip)
        home = asked_of(orders_ref, ks[0]) // CORES
        has = (hop >= 1) & ((home == chip) | ((core == 0) == (home < chip)))
        half = 1 - core if apart else core
        lead = jnp.maximum(hop, 1) - 1
        for j in range(chips - 1):

            @pl.when((lead == j) & (lead == j if apart else has))
            def _(j=j):
                for m, k in enumerate(ks):
                    pltpu.make_async_copy(ins[slots[k, j]].at[half], outs[m], sems.at[m]).start()

        if not apart:

            @pl.when(jnp.logical_not(has))
            def _():
                for m in range(len(ks)):
                    pltpu.make_async_copy(refs[len(arrays) + m], outs[m], sems.at[m]).start()

        for m in range(len(ks)):
            pltpu.make_async_copy(outs[m], outs[m], sems.at[m]).wait()

    in_vmem = pl.BlockSpec(memory_space=pltpu.VMEM)
    if apart:
        out_specs, out_shape = [in_vmem] * len(ks), [jax.ShapeDtypeStruct(shape, jnp.bfloat16)] * len(ks)
    else:
        out_specs, out_shape = [in_vmem], [jax.ShapeDtypeStruct((len(ks), *shape), jnp.bfloat16)]
    return pl.pallas_call(
        kernel,
        in_specs=[pl.BlockSpec(memory_space=pltpu.SMEM)] + [in_place()] * (len(arrays) + len(extra) + 1),
        out_specs=out_specs + [in_place()],
        out_shape=out_shape + [token_shape()],
        scratch_shapes=[pltpu.SemaphoreType.DMA((len(ks),))],
        name="collect" if apart else "select",
        compiler_params=pltpu.CompilerParams(vmem_limit_bytes=8 * 2**20),
        cost_estimate=SHORT,
    )(orders, *arrays, *extra, token)


def cross_kernel(core_ref, own_ref, near_ref, far_ref, *refs):
    out_ref = refs[-2]

    def emit(paired_ref):
        own = own_ref[0, 0]
        turned = jnp.concatenate([own[:, WIN:], -own[:, :WIN]], axis=1)
        both = jnp.concatenate([own, turned], axis=0)
        paired = paired_ref[0].reshape(2 * WIN, -1)
        total = jnp.dot(both, paired, preferred_element_type=jnp.float32) * (1.0 / math.sqrt(WIN))
        out_ref[0, :, 0] = total.astype(jnp.bfloat16).reshape(2, *out_ref.shape[3:])

    @pl.when(pl.program_id(1) == 0)
    def _():
        emit(near_ref)

    @pl.when(pl.program_id(1) == 1)
    def _():
        emit(far_ref)


def cross(out, token, core, own, near, far, round_index, first_chunk, begin, count):
    channels = near.shape[-1]
    first_chunk += begin
    row = first_chunk % own.shape[0]
    paired_spec = pl.BlockSpec((1, 2, WIN, channels), lambda i, g, c: (begin + i, 0, 0, 0))
    in_specs = [
        pl.BlockSpec((1, 1, channels, 2 * WIN), lambda i, g, c: (row + i, (c[0] + g) % CORES, 0, 0)),
        paired_spec,
        paired_spec,
        in_place(),
    ]
    out_spec = pl.BlockSpec(
        (1, 2, 1, channels, channels),
        lambda i, g, c: (round_index, 0, ((c[0] + g) % CORES) * HALF + first_chunk + i, 0, 0),
    )
    args = [core, own, near, far, token]
    aliases = {}
    if out is not None:
        in_specs.append(in_place())
        args.append(out)
        aliases = {len(args) - 1: 0}
    return pl.pallas_call(
        cross_kernel,
        grid_spec=pltpu.PrefetchScalarGridSpec(
            num_scalar_prefetch=1, grid=(count, CORES), in_specs=in_specs, out_specs=[out_spec, in_place()]
        ),
        out_shape=[jax.ShapeDtypeStruct((ROUNDS, 2, NB, channels, channels), jnp.bfloat16), token_shape()],
        input_output_aliases=aliases,
        name="cross",
        compiler_params=pltpu.CompilerParams(vmem_limit_bytes=VMEM),
        cost_estimate=SHORT,
    )(*args)


def body(record, owner_order):
    groups, members = lax.axis_size("blk"), lax.axis_size("grp")
    chips = members // CORES
    core_arg = (lax.axis_index("grp") % CORES).reshape(1).astype(jnp.int32)

    flow = [(m, m + CORES) for m in range(0, members - CORES, CORES)]
    flow += [(m + CORES, m) for m in range(1, members - CORES, CORES)]
    swap = [(m, m ^ 1) for m in range(members)]
    chunks = ROUNDS * HALF
    steps = chunks + LAG * (chips - 2)

    mine_a, inv, token = band(core_arg, record, 0, FIRST)
    mine, twin = [mine_a], [lax.ppermute(mine_a[i], "grp", swap) for i in range(FIRST)]

    arrived, held, turned = [], [], []
    out = None
    kept, nears, fars = {}, {}, {}
    todo = {}
    for g in range(chunks // GROUP):
        at = (g + 1) * GROUP - 1 + LAG * (chips - 2) + LAG
        across = bool(ORDER[g][0])
        left = chunks // GROUP - 1 - g
        pick = at + (1 if left == 0 else PICK)
        give = pick + GIVE if across else pick
        meet = at + TAIL[left] if left < 4 else give + GAP
        plan = ((at, "collect", 0), (pick, "select", 0), (give, "pass_over", 0), *((meet + i * (left >= 4), "cross", i) for i in range(PARTS)))
        for wait, what, part in plan:
            todo.setdefault(wait, []).append((what, g, part))

    for step in range(max(todo) + 1):
        if step < steps + LAG:
            buffer = arrived[step - LAG] if step >= LAG else None
            sent, token = inject(owner_order, token, step, mine, twin, buffer)
            if step < steps:
                arrived.append(lax.ppermute(sent, "grp", flow))
            if step >= LAG:
                held.append(sent)
        if step == REST_AT:
            mine_b, token = band(core_arg, record, FIRST, HALF, inv, token)
            mine.append(mine_b)
            twin += [lax.ppermute(mine_b[i], "grp", swap) for i in range(HALF - FIRST)]
        if step in TURN:
            part, token = turn(mine[TURN.index(step)], token)
            turned.append(part)
        for what, g, part in sorted(todo.get(step, ()), key=lambda item: item[0] in ("pass_over", "cross")):
            first = g * GROUP
            ks = range(first, first + GROUP)
            r, begin = chunk_of(first)
            if what == "collect":
                *given, token = gather(owner_order, token, ks, held)
                kept[g] = [lax.ppermute(x, "grp", swap) for x in given]
            elif what == "select":
                near, token = gather(owner_order, token, ks, held, kept[g])
                if r:
                    near = lax.ppermute(near, "blk", [(b, (b + r) % groups) for b in range(groups)])
                nears[g] = near
            elif what == "pass_over":
                fars[g] = lax.ppermute(nears[g], "grp", swap)
            else:
                own, count = turned[begin // FIRST], GROUP // PARTS
                out, token = cross(out, token, core_arg, own, nears[g], fars[g], r, begin, part * count, count)
    return out


def solution(mesh):
    return jax.shard_map(
        body,
        mesh=mesh,
        in_specs=(P(None, ("blk", "grp")), P()),
        out_specs=P(None, None, None, ("blk", "grp"), None),
        check_vma=False,
    )
```

```python
import functools
import math

import jax
import jax.numpy as jnp
import numpy as np
from jax import lax
from jax.experimental import pallas as pl
from jax.experimental.pallas import tpu as pltpu
from jax.sharding import PartitionSpec as P

WIN = 256
NS = 128
NB = 16
BIN_LO = 8
ROUNDS = 4
HOP = 64
WG = 16
CORES = 2
HALF = NB // CORES
FIRST = 4
GROUP = 4
PICK = 3
GIVE = 5
TAIL = (2, 5, 9, 11)
PARTS, TURN = 2, (5, 7)
GAP = 5
REST_AT = 1
LAG = 2
ORDER = ((1, 0), (1, 1), (3, 0), (3, 1), (2, 0), (2, 1), (0, 0), (0, 1))
VMEM = 8 * 2**20
SHORT = pl.CostEstimate(flops=1, bytes_accessed=1, transcendentals=0)


def band_table():
    n = np.arange(NS)
    q = BIN_LO + np.arange(NB)
    phase = ((q[:, None] * n[None, :]) % NS) * (2.0 * math.pi / NS)
    taper = 0.5 - 0.5 * np.cos(n * (2.0 * math.pi / NS))
    scale = 1.0 / math.sqrt(3.0 * NS / 8.0)
    real = taper * np.cos(phase) * scale
    imag = -taper * np.sin(phase) * scale
    return np.stack([real, imag], axis=1).astype(np.float32)


def tables(lo, hi):
    table = band_table().reshape(CORES, HALF, 2, NS)[:, lo:hi].swapaxes(0, 1)
    out = np.stack([np.roll(table, w * HOP, axis=-1) for w in range(WG)], axis=-2)
    return jnp.asarray(out.reshape(-1, NS).astype(jnp.bfloat16))


def in_hbm():
    return pl.BlockSpec(memory_space=pltpu.MemorySpace.HBM)


def token_shape():
    return jax.ShapeDtypeStruct((8, 128), jnp.int32)


def in_place():
    return pl.BlockSpec(memory_space=pl.ANY)


def half_energy(x):
    wide = x.astype(jnp.float32)
    return jnp.sum((wide * wide).reshape(-1, HOP, x.shape[-1]), axis=1)


def band_kernel(first, core_ref, main_ref, halo_ref, rows_ref, *refs):
    *refs, table = refs

    @pl.when(pl.program_id(0) == 0)
    def _():
        rows = rows_ref[...].astype(jnp.float32)
        start = (lax.broadcasted_iota(jnp.int32, rows.shape, 0) & (WG - 1)) * HOP
        lane = lax.broadcasted_iota(jnp.int32, rows.shape, 1)
        for at in range(0, table.shape[1], NS):
            sample = lane + at - start
            table[:, at : at + NS] = jnp.where((sample >= 0) & (sample < NS), rows, 0.0).astype(jnp.bfloat16)

    main, halo = main_ref[...], halo_ref[...]
    if first:
        out, inv_ref, _ = refs
        energy = half_energy(main)
        later = jnp.concatenate([energy[1:], half_energy(halo)], axis=0)
        inv = 1.0 / jnp.sqrt((energy + later) / NS + 1e-05)
        inv_ref[...] = inv
    else:
        inv_ref, _, out, _ = refs
        inv = inv_ref[...]
    split = WG * HOP
    raw = jnp.dot(table[:, :split], main, preferred_element_type=jnp.float32)
    raw += jnp.dot(table[:, split : split + HOP], halo, preferred_element_type=jnp.float32)
    raw = raw.reshape(-1, CORES, 2, WG, main.shape[1])
    out[...] = (raw * inv).astype(jnp.bfloat16)


def band(core, record, lo, hi, inv=None, token=None):
    channels = record.shape[1]
    table = tables(lo, hi)
    rows, width = table.shape[0], (WG // 2 + 1) * NS
    first = inv is None
    inv_spec = pl.BlockSpec((WG, channels), lambda i: (i, 0))
    in_specs = [
        pl.BlockSpec(memory_space=pltpu.SMEM),
        pl.BlockSpec((WG * HOP, channels), lambda i: (i, 0)),
        pl.BlockSpec((HOP, channels), lambda i: ((i + 1) * WG, 0)),
        pl.BlockSpec(table.shape, lambda i: (0, 0)),
    ]
    out_specs = [pl.BlockSpec((hi - lo, CORES, 2, WG, channels), lambda i: (0, 0, 0, i, 0))]
    out_shape = [jax.ShapeDtypeStruct((hi - lo, CORES, 2, WIN, channels), jnp.bfloat16)]
    args = [core, record, record, table]
    if first:
        out_specs.append(inv_spec)
        out_shape.append(jax.ShapeDtypeStruct((WIN, channels), jnp.float32))
    else:
        in_specs += [inv_spec, in_place()]
        args += [inv, token]
    return pl.pallas_call(
        functools.partial(band_kernel, first),
        grid=(WIN // WG,),
        in_specs=in_specs,
        out_specs=out_specs + [in_place()],
        out_shape=out_shape + [token_shape()],
        scratch_shapes=[pltpu.VMEM((rows, width), jnp.bfloat16)],
        name="band_first" if first else "band_rest",
        compiler_params=pltpu.CompilerParams(vmem_limit_bytes=VMEM),
        cost_estimate=pl.CostEstimate(
            flops=2 * rows * (WIN // WG) * width * channels, bytes_accessed=3 * record.size, transcendentals=0
        ),
    )(*args)


def turn_kernel(in_ref, _, out_ref, __):
    for part in range(2):
        out_ref[0, 0, :, part * WIN : (part + 1) * WIN] = in_ref[0, 0, part].T


def turn(spectra, token):
    count, channels = spectra.shape[0], spectra.shape[-1]
    return pl.pallas_call(
        turn_kernel,
        grid=(count, CORES),
        in_specs=[pl.BlockSpec((1, 1, 2, WIN, channels), lambda i, h: (i, h, 0, 0, 0)), in_place()],
        out_specs=[pl.BlockSpec((1, 1, channels, 2 * WIN), lambda i, h: (i, h, 0, 0)), in_place()],
        out_shape=[jax.ShapeDtypeStruct((count, CORES, channels, 2 * WIN), jnp.bfloat16), token_shape()],
        name="turn",
        compiler_params=pltpu.CompilerParams(vmem_limit_bytes=VMEM),
        cost_estimate=SHORT,
    )(spectra, token)


def place(arrays, a):
    for i, b in enumerate(arrays):
        if b is a:
            return i
    arrays.append(a)
    return len(arrays) - 1


def seat():
    member = lax.axis_index("grp")
    return lax.axis_index("blk"), member // CORES, member % CORES, lax.axis_size("grp") // CORES


def chunk_of(k):
    r, half = ORDER[k // GROUP]
    return r, half * GROUP + k % GROUP


def asked_of(orders, k):
    r, _ = chunk_of(k)
    return orders[r, lax.rem(lax.axis_index("blk") + r, lax.axis_size("blk"))]


def inject(orders, token, step, mine, twin, held):
    chips = lax.axis_size("grp") // CORES
    sent = [step - LAG * hop for hop in range(chips)]
    hops = [hop for hop in range(chips) if 0 <= sent[hop] < ROUNDS * HALF]
    arrays, slots = [], {}
    for hop in hops:
        _, row = chunk_of(sent[hop])
        slots[hop] = (place(arrays, mine[row // FIRST]), row % FIRST), (place(arrays, twin[row]), None)
    whole = twin[0].shape

    def kernel(orders_ref, *refs):
        ins, out, buffer, sem = refs[: len(arrays)], refs[-4], refs[-2], refs[-1]
        _, chip, core, _ = seat()
        seen = jnp.where(core == 0, chip, chips - 1 - chip)
        for hop in hops:
            owner = asked_of(orders_ref, sent[hop])
            here = (seen == hop) & (owner // CORES == chip)
            for (slot, row), same in zip(slots[hop], (True, False), strict=True):
                source = ins[slot] if row is None else ins[slot].at[row]

                @pl.when(here & ((owner % CORES == core) == same))
                def _(source=source):
                    load = pltpu.make_async_copy(source, buffer, sem.at[0])
                    load.start()
                    load.wait()
                    store = pltpu.make_async_copy(buffer, out, sem.at[1])
                    store.start()
                    store.wait()

    in_specs = [pl.BlockSpec(memory_space=pltpu.SMEM)] + [in_hbm()] * len(arrays) + [in_place()]
    args = [orders, *arrays, token]
    aliases = {}
    if held is not None:
        in_specs.append(in_place())
        args.append(held)
        aliases = {len(args) - 1: 0}
    return pl.pallas_call(
        kernel,
        in_specs=in_specs,
        out_specs=[in_place()] * 2,
        out_shape=[jax.ShapeDtypeStruct(whole, jnp.bfloat16), token_shape()],
        input_output_aliases=aliases,
        scratch_shapes=[pltpu.VMEM(whole, jnp.bfloat16), pltpu.SemaphoreType.DMA((2,))],
        name="inject",
        compiler_params=pltpu.CompilerParams(vmem_limit_bytes=4 * 2**20),
        cost_estimate=SHORT,
    )(*args)


def gather(orders, token, ks, held, swapped=None):
    arrays = []
    chips = lax.axis_size("grp") // CORES
    slots = {(k, j): place(arrays, held[k + LAG * j]) for k in ks for j in range(chips - 1)}
    extra = [] if swapped is None else swapped
    apart = swapped is None
    shape = held[0].shape[1:]

    def kernel(orders_ref, *refs):
        ins, sems = refs[: len(arrays)], refs[-1]
        outs = refs[-2 - len(ks) : -2] if apart else [refs[-3].at[m] for m in range(len(ks))]
        _, chip, core, _ = seat()
        hop = jnp.where(core == 0, chip, chips - 1 - chip)
        home = asked_of(orders_ref, ks[0]) // CORES
        has = (hop >= 1) & ((home == chip) | ((core == 0) == (home < chip)))
        half = 1 - core if apart else core
        lead = jnp.maximum(hop, 1) - 1
        for j in range(chips - 1):

            @pl.when((lead == j) & (lead == j if apart else has))
            def _(j=j):
                for m, k in enumerate(ks):
                    pltpu.make_async_copy(ins[slots[k, j]].at[half], outs[m], sems.at[m]).start()

        if not apart:

            @pl.when(jnp.logical_not(has))
            def _():
                for m in range(len(ks)):
                    pltpu.make_async_copy(refs[len(arrays) + m], outs[m], sems.at[m]).start()

        for m in range(len(ks)):
            pltpu.make_async_copy(outs[m], outs[m], sems.at[m]).wait()

    in_vmem = pl.BlockSpec(memory_space=pltpu.VMEM)
    if apart:
        out_specs, out_shape = [in_vmem] * len(ks), [jax.ShapeDtypeStruct(shape, jnp.bfloat16)] * len(ks)
    else:
        out_specs, out_shape = [in_vmem], [jax.ShapeDtypeStruct((len(ks), *shape), jnp.bfloat16)]
    return pl.pallas_call(
        kernel,
        in_specs=[pl.BlockSpec(memory_space=pltpu.SMEM)] + [in_place()] * (len(arrays) + len(extra) + 1),
        out_specs=out_specs + [in_place()],
        out_shape=out_shape + [token_shape()],
        scratch_shapes=[pltpu.SemaphoreType.DMA((len(ks),))],
        name="collect" if apart else "select",
        compiler_params=pltpu.CompilerParams(vmem_limit_bytes=8 * 2**20),
        cost_estimate=SHORT,
    )(orders, *arrays, *extra, token)


def cross_kernel(core_ref, own_ref, near_ref, far_ref, *refs):
    out_ref = refs[-2]

    def emit(paired_ref):
        own = own_ref[0, 0]
        turned = jnp.concatenate([own[:, WIN:], -own[:, :WIN]], axis=1)
        both = jnp.concatenate([own, turned], axis=0)
        paired = paired_ref[0].reshape(2 * WIN, -1)
        total = jnp.dot(both, paired, preferred_element_type=jnp.float32) * (1.0 / math.sqrt(WIN))
        out_ref[0, :, 0] = total.astype(jnp.bfloat16).reshape(2, *out_ref.shape[3:])

    @pl.when(pl.program_id(1) == 0)
    def _():
        emit(near_ref)

    @pl.when(pl.program_id(1) == 1)
    def _():
        emit(far_ref)


def cross(out, token, core, own, near, far, round_index, first_chunk, begin, count):
    channels = near.shape[-1]
    first_chunk += begin
    row = first_chunk % own.shape[0]
    paired_spec = pl.BlockSpec((1, 2, WIN, channels), lambda i, g, c: (begin + i, 0, 0, 0))
    in_specs = [
        pl.BlockSpec((1, 1, channels, 2 * WIN), lambda i, g, c: (row + i, (c[0] + g) % CORES, 0, 0)),
        paired_spec,
        paired_spec,
        in_place(),
    ]
    out_spec = pl.BlockSpec(
        (1, 2, 1, channels, channels),
        lambda i, g, c: (round_index, 0, ((c[0] + g) % CORES) * HALF + first_chunk + i, 0, 0),
    )
    args = [core, own, near, far, token]
    aliases = {}
    if out is not None:
        in_specs.append(in_place())
        args.append(out)
        aliases = {len(args) - 1: 0}
    return pl.pallas_call(
        cross_kernel,
        grid_spec=pltpu.PrefetchScalarGridSpec(
            num_scalar_prefetch=1, grid=(count, CORES), in_specs=in_specs, out_specs=[out_spec, in_place()]
        ),
        out_shape=[jax.ShapeDtypeStruct((ROUNDS, 2, NB, channels, channels), jnp.bfloat16), token_shape()],
        input_output_aliases=aliases,
        name="cross",
        compiler_params=pltpu.CompilerParams(vmem_limit_bytes=VMEM),
        cost_estimate=SHORT,
    )(*args)


def body(record, owner_order):
    groups, members = lax.axis_size("blk"), lax.axis_size("grp")
    chips = members // CORES
    core_arg = (lax.axis_index("grp") % CORES).reshape(1).astype(jnp.int32)

    flow = [(m, m + CORES) for m in range(0, members - CORES, CORES)]
    flow += [(m + CORES, m) for m in range(1, members - CORES, CORES)]
    swap = [(m, m ^ 1) for m in range(members)]
    chunks = ROUNDS * HALF
    steps = chunks + LAG * (chips - 2)

    mine_a, inv, token = band(core_arg, record, 0, FIRST)
    mine, twin = [mine_a], [lax.ppermute(mine_a[i], "grp", swap) for i in range(FIRST)]

    arrived, held, turned = [], [], []
    out = None
    kept, nears, fars = {}, {}, {}
    todo = {}
    for g in range(chunks // GROUP):
        at = (g + 1) * GROUP - 1 + LAG * (chips - 2) + LAG
        across = bool(ORDER[g][0])
        left = chunks // GROUP - 1 - g
        pick = at + (1 if left == 0 else PICK)
        give = pick + GIVE if across else pick
        meet = at + TAIL[left] if left < 4 else give + GAP
        plan = ((at, "collect", 0), (pick, "select", 0), (give, "pass_over", 0), *((meet + i * (left >= 4), "cross", i) for i in range(PARTS)))
        for wait, what, part in plan:
            todo.setdefault(wait, []).append((what, g, part))

    for step in range(max(todo) + 1):
        if step < steps + LAG:
            buffer = arrived[step - LAG] if step >= LAG else None
            sent, token = inject(owner_order, token, step, mine, twin, buffer)
            if step < steps:
                arrived.append(lax.ppermute(sent, "grp", flow))
            if step >= LAG:
                held.append(sent)
        if step == REST_AT:
            mine_b, token = band(core_arg, record, FIRST, HALF, inv, token)
            mine.append(mine_b)
            twin += [lax.ppermute(mine_b[i], "grp", swap) for i in range(HALF - FIRST)]
        if step in TURN:
            part, token = turn(mine[TURN.index(step)], token)
            turned.append(part)
        for what, g, part in sorted(todo.get(step, ()), key=lambda item: item[0] in ("pass_over", "cross")):
            first = g * GROUP
            ks = range(first, first + GROUP)
            r, begin = chunk_of(first)
            if what == "collect":
                *given, token = gather(owner_order, token, ks, held)
                kept[g] = [lax.ppermute(x, "grp", swap) for x in given]
            elif what == "select":
                near, token = gather(owner_order, token, ks, held, kept[g])
                if r:
                    near = lax.ppermute(near, "blk", [(b, (b + r) % groups) for b in range(groups)])
                nears[g] = near
            elif what == "pass_over":
                fars[g] = lax.ppermute(nears[g], "grp", swap)
            else:
                own, count = turned[begin // FIRST], GROUP // PARTS
                out, token = cross(out, token, core_arg, own, nears[g], fars[g], r, begin, part * count, count)
    return out


def solution(mesh):
    return jax.shard_map(
        body,
        mesh=mesh,
        in_specs=(P(None, ("blk", "grp")), P()),
        out_specs=P(None, None, None, ("blk", "grp"), None),
        check_vma=False,
    )
```

```python
import functools
import math

import jax
import jax.numpy as jnp
import numpy as np
from jax import lax
from jax.experimental import pallas as pl
from jax.experimental.pallas import tpu as pltpu
from jax.sharding import PartitionSpec as P

WIN = 256
NS = 128
NB = 16
BIN_LO = 8
ROUNDS = 4
HOP = 64
WG = 16
CORES = 2
HALF = NB // CORES
FIRST = 4
GROUP = 4
PICK = 3
GIVE = 5
TAIL = (2, 5, 9, 11)
PARTS, TURN = 2, (5, 7)
GAP = 5
REST_AT = 1
LAG = 2
ORDER = ((1, 0), (1, 1), (3, 0), (3, 1), (2, 0), (2, 1), (0, 0), (0, 1))
VMEM = 8 * 2**20
SHORT = pl.CostEstimate(flops=1, bytes_accessed=1, transcendentals=0)


def band_table():
    n = np.arange(NS)
    q = BIN_LO + np.arange(NB)
    phase = ((q[:, None] * n[None, :]) % NS) * (2.0 * math.pi / NS)
    taper = 0.5 - 0.5 * np.cos(n * (2.0 * math.pi / NS))
    scale = 1.0 / math.sqrt(3.0 * NS / 8.0)
    real = taper * np.cos(phase) * scale
    imag = -taper * np.sin(phase) * scale
    return np.stack([real, imag], axis=1).astype(np.float32)


def tables(lo, hi):
    table = band_table().reshape(CORES, HALF, 2, NS)[:, lo:hi].swapaxes(0, 1)
    out = np.stack([np.roll(table, w * HOP, axis=-1) for w in range(WG)], axis=-2)
    return jnp.asarray(out.reshape(-1, NS).astype(jnp.bfloat16))


def in_hbm():
    return pl.BlockSpec(memory_space=pltpu.MemorySpace.HBM)


def token_shape():
    return jax.ShapeDtypeStruct((8, 128), jnp.int32)


def in_place():
    return pl.BlockSpec(memory_space=pl.ANY)


def half_energy(x):
    wide = x.astype(jnp.float32)
    return jnp.sum((wide * wide).reshape(-1, HOP, x.shape[-1]), axis=1)


def band_kernel(first, core_ref, main_ref, halo_ref, rows_ref, *refs):
    *refs, table = refs

    @pl.when(pl.program_id(0) == 0)
    def _():
        rows = rows_ref[...].astype(jnp.float32)
        start = (lax.broadcasted_iota(jnp.int32, rows.shape, 0) & (WG - 1)) * HOP
        lane = lax.broadcasted_iota(jnp.int32, rows.shape, 1)
        for at in range(0, table.shape[1], NS):
            sample = lane + at - start
            table[:, at : at + NS] = jnp.where((sample >= 0) & (sample < NS), rows, 0.0).astype(jnp.bfloat16)

    main, halo = main_ref[...], halo_ref[...]
    if first:
        out, inv_ref, _ = refs
        energy = half_energy(main)
        later = jnp.concatenate([energy[1:], half_energy(halo)], axis=0)
        inv = 1.0 / jnp.sqrt((energy + later) / NS + 1e-05)
        inv_ref[...] = inv
    else:
        inv_ref, _, out, _ = refs
        inv = inv_ref[...]
    split = WG * HOP
    raw = jnp.dot(table[:, :split], main, preferred_element_type=jnp.float32)
    raw += jnp.dot(table[:, split : split + HOP], halo, preferred_element_type=jnp.float32)
    raw = raw.reshape(-1, CORES, 2, WG, main.shape[1])
    out[...] = (raw * inv).astype(jnp.bfloat16)


def band(core, record, lo, hi, inv=None, token=None):
    channels = record.shape[1]
    table = tables(lo, hi)
    rows, width = table.shape[0], (WG // 2 + 1) * NS
    first = inv is None
    inv_spec = pl.BlockSpec((WG, channels), lambda i: (i, 0))
    in_specs = [
        pl.BlockSpec(memory_space=pltpu.SMEM),
        pl.BlockSpec((WG * HOP, channels), lambda i: (i, 0)),
        pl.BlockSpec((HOP, channels), lambda i: ((i + 1) * WG, 0)),
        pl.BlockSpec(table.shape, lambda i: (0, 0)),
    ]
    out_specs = [pl.BlockSpec((hi - lo, CORES, 2, WG, channels), lambda i: (0, 0, 0, i, 0))]
    out_shape = [jax.ShapeDtypeStruct((hi - lo, CORES, 2, WIN, channels), jnp.bfloat16)]
    args = [core, record, record, table]
    if first:
        out_specs.append(inv_spec)
        out_shape.append(jax.ShapeDtypeStruct((WIN, channels), jnp.float32))
    else:
        in_specs += [inv_spec, in_place()]
        args += [inv, token]
    return pl.pallas_call(
        functools.partial(band_kernel, first),
        grid=(WIN // WG,),
        in_specs=in_specs,
        out_specs=out_specs + [in_place()],
        out_shape=out_shape + [token_shape()],
        scratch_shapes=[pltpu.VMEM((rows, width), jnp.bfloat16)],
        name="band_first" if first else "band_rest",
        compiler_params=pltpu.CompilerParams(vmem_limit_bytes=VMEM),
        cost_estimate=pl.CostEstimate(
            flops=2 * rows * (WIN // WG) * width * channels, bytes_accessed=3 * record.size, transcendentals=0
        ),
    )(*args)


def turn_kernel(in_ref, _, out_ref, __):
    for part in range(2):
        out_ref[0, 0, :, part * WIN : (part + 1) * WIN] = in_ref[0, 0, part].T


def turn(spectra, token):
    count, channels = spectra.shape[0], spectra.shape[-1]
    return pl.pallas_call(
        turn_kernel,
        grid=(count, CORES),
        in_specs=[pl.BlockSpec((1, 1, 2, WIN, channels), lambda i, h: (i, h, 0, 0, 0)), in_place()],
        out_specs=[pl.BlockSpec((1, 1, channels, 2 * WIN), lambda i, h: (i, h, 0, 0)), in_place()],
        out_shape=[jax.ShapeDtypeStruct((count, CORES, channels, 2 * WIN), jnp.bfloat16), token_shape()],
        name="turn",
        compiler_params=pltpu.CompilerParams(vmem_limit_bytes=VMEM),
        cost_estimate=SHORT,
    )(spectra, token)


def place(arrays, a):
    for i, b in enumerate(arrays):
        if b is a:
            return i
    arrays.append(a)
    return len(arrays) - 1


def seat():
    member = lax.axis_index("grp")
    return lax.axis_index("blk"), member // CORES, member % CORES, lax.axis_size("grp") // CORES


def chunk_of(k):
    r, half = ORDER[k // GROUP]
    return r, half * GROUP + k % GROUP


def asked_of(orders, k):
    r, _ = chunk_of(k)
    return orders[r, lax.rem(lax.axis_index("blk") + r, lax.axis_size("blk"))]


def inject(orders, token, step, mine, twin, held):
    chips = lax.axis_size("grp") // CORES
    sent = [step - LAG * hop for hop in range(chips)]
    hops = [hop for hop in range(chips) if 0 <= sent[hop] < ROUNDS * HALF]
    arrays, slots = [], {}
    for hop in hops:
        _, row = chunk_of(sent[hop])
        slots[hop] = (place(arrays, mine[row // FIRST]), row % FIRST), (place(arrays, twin[row]), None)
    whole = twin[0].shape

    def kernel(orders_ref, *refs):
        ins, out, buffer, sem = refs[: len(arrays)], refs[-4], refs[-2], refs[-1]
        _, chip, core, _ = seat()
        seen = jnp.where(core == 0, chip, chips - 1 - chip)
        for hop in hops:
            owner = asked_of(orders_ref, sent[hop])
            here = (seen == hop) & (owner // CORES == chip)
            for (slot, row), same in zip(slots[hop], (True, False), strict=True):
                source = ins[slot] if row is None else ins[slot].at[row]

                @pl.when(here & ((owner % CORES == core) == same))
                def _(source=source):
                    load = pltpu.make_async_copy(source, buffer, sem.at[0])
                    load.start()
                    load.wait()
                    store = pltpu.make_async_copy(buffer, out, sem.at[1])
                    store.start()
                    store.wait()

    in_specs = [pl.BlockSpec(memory_space=pltpu.SMEM)] + [in_hbm()] * len(arrays) + [in_place()]
    args = [orders, *arrays, token]
    aliases = {}
    if held is not None:
        in_specs.append(in_place())
        args.append(held)
        aliases = {len(args) - 1: 0}
    return pl.pallas_call(
        kernel,
        in_specs=in_specs,
        out_specs=[in_place()] * 2,
        out_shape=[jax.ShapeDtypeStruct(whole, jnp.bfloat16), token_shape()],
        input_output_aliases=aliases,
        scratch_shapes=[pltpu.VMEM(whole, jnp.bfloat16), pltpu.SemaphoreType.DMA((2,))],
        name="inject",
        compiler_params=pltpu.CompilerParams(vmem_limit_bytes=4 * 2**20),
        cost_estimate=SHORT,
    )(*args)


def gather(orders, token, ks, held, swapped=None):
    arrays = []
    chips = lax.axis_size("grp") // CORES
    slots = {(k, j): place(arrays, held[k + LAG * j]) for k in ks for j in range(chips - 1)}
    extra = [] if swapped is None else swapped
    apart = swapped is None
    shape = held[0].shape[1:]

    def kernel(orders_ref, *refs):
        ins, sems = refs[: len(arrays)], refs[-1]
        outs = refs[-2 - len(ks) : -2] if apart else [refs[-3].at[m] for m in range(len(ks))]
        _, chip, core, _ = seat()
        hop = jnp.where(core == 0, chip, chips - 1 - chip)
        home = asked_of(orders_ref, ks[0]) // CORES
        has = (hop >= 1) & ((home == chip) | ((core == 0) == (home < chip)))
        half = 1 - core if apart else core
        lead = jnp.maximum(hop, 1) - 1
        for j in range(chips - 1):

            @pl.when((lead == j) & (lead == j if apart else has))
            def _(j=j):
                for m, k in enumerate(ks):
                    pltpu.make_async_copy(ins[slots[k, j]].at[half], outs[m], sems.at[m]).start()

        if not apart:

            @pl.when(jnp.logical_not(has))
            def _():
                for m in range(len(ks)):
                    pltpu.make_async_copy(refs[len(arrays) + m], outs[m], sems.at[m]).start()

        for m in range(len(ks)):
            pltpu.make_async_copy(outs[m], outs[m], sems.at[m]).wait()

    in_vmem = pl.BlockSpec(memory_space=pltpu.VMEM)
    if apart:
        out_specs, out_shape = [in_vmem] * len(ks), [jax.ShapeDtypeStruct(shape, jnp.bfloat16)] * len(ks)
    else:
        out_specs, out_shape = [in_vmem], [jax.ShapeDtypeStruct((len(ks), *shape), jnp.bfloat16)]
    return pl.pallas_call(
        kernel,
        in_specs=[pl.BlockSpec(memory_space=pltpu.SMEM)] + [in_place()] * (len(arrays) + len(extra) + 1),
        out_specs=out_specs + [in_place()],
        out_shape=out_shape + [token_shape()],
        scratch_shapes=[pltpu.SemaphoreType.DMA((len(ks),))],
        name="collect" if apart else "select",
        compiler_params=pltpu.CompilerParams(vmem_limit_bytes=8 * 2**20),
        cost_estimate=SHORT,
    )(orders, *arrays, *extra, token)


def cross_kernel(core_ref, own_ref, near_ref, far_ref, *refs):
    out_ref = refs[-2]

    def emit(paired_ref):
        own = own_ref[0, 0]
        turned = jnp.concatenate([own[:, WIN:], -own[:, :WIN]], axis=1)
        paired = paired_ref[0].reshape(2 * WIN, -1)
        scale = 1.0 / math.sqrt(WIN)
        for part, lhs in enumerate((own, turned)):
            total = jnp.dot(lhs, paired, preferred_element_type=jnp.float32)
            out_ref[0, part, 0] = (total * scale).astype(jnp.bfloat16)

    @pl.when(pl.program_id(1) == 0)
    def _():
        emit(near_ref)

    @pl.when(pl.program_id(1) == 1)
    def _():
        emit(far_ref)


def cross(out, token, core, own, near, far, round_index, first_chunk, begin, count):
    channels = near.shape[-1]
    first_chunk += begin
    row = first_chunk % own.shape[0]
    paired_spec = pl.BlockSpec((1, 2, WIN, channels), lambda i, g, c: (begin + i, 0, 0, 0))
    in_specs = [
        pl.BlockSpec((1, 1, channels, 2 * WIN), lambda i, g, c: (row + i, (c[0] + g) % CORES, 0, 0)),
        paired_spec,
        paired_spec,
        in_place(),
    ]
    out_spec = pl.BlockSpec(
        (1, 2, 1, channels, channels),
        lambda i, g, c: (round_index, 0, ((c[0] + g) % CORES) * HALF + first_chunk + i, 0, 0),
    )
    args = [core, own, near, far, token]
    aliases = {}
    if out is not None:
        in_specs.append(in_place())
        args.append(out)
        aliases = {len(args) - 1: 0}
    return pl.pallas_call(
        cross_kernel,
        grid_spec=pltpu.PrefetchScalarGridSpec(
            num_scalar_prefetch=1, grid=(count, CORES), in_specs=in_specs, out_specs=[out_spec, in_place()]
        ),
        out_shape=[jax.ShapeDtypeStruct((ROUNDS, 2, NB, channels, channels), jnp.bfloat16), token_shape()],
        input_output_aliases=aliases,
        name="cross",
        compiler_params=pltpu.CompilerParams(vmem_limit_bytes=VMEM),
        cost_estimate=SHORT,
    )(*args)


def body(record, owner_order):
    groups, members = lax.axis_size("blk"), lax.axis_size("grp")
    chips = members // CORES
    core_arg = (lax.axis_index("grp") % CORES).reshape(1).astype(jnp.int32)

    flow = [(m, m + CORES) for m in range(0, members - CORES, CORES)]
    flow += [(m + CORES, m) for m in range(1, members - CORES, CORES)]
    swap = [(m, m ^ 1) for m in range(members)]
    chunks = ROUNDS * HALF
    steps = chunks + LAG * (chips - 2)

    mine_a, inv, token = band(core_arg, record, 0, FIRST)
    mine, twin = [mine_a], [lax.ppermute(mine_a[i], "grp", swap) for i in range(FIRST)]

    arrived, held, turned = [], [], []
    out = None
    kept, nears, fars = {}, {}, {}
    todo = {}
    for g in range(chunks // GROUP):
        at = (g + 1) * GROUP - 1 + LAG * (chips - 2) + LAG
        across = bool(ORDER[g][0])
        left = chunks // GROUP - 1 - g
        pick = at + (1 if left == 0 else PICK)
        give = pick + GIVE if across else pick
        meet = at + TAIL[left] if left < 4 else give + GAP
        plan = ((at, "collect", 0), (pick, "select", 0), (give, "pass_over", 0), *((meet + i * (left >= 4), "cross", i) for i in range(PARTS)))
        for wait, what, part in plan:
            todo.setdefault(wait, []).append((what, g, part))

    for step in range(max(todo) + 1):
        if step < steps + LAG:
            buffer = arrived[step - LAG] if step >= LAG else None
            sent, token = inject(owner_order, token, step, mine, twin, buffer)
            if step < steps:
                arrived.append(lax.ppermute(sent, "grp", flow))
            if step >= LAG:
                held.append(sent)
        if step == REST_AT:
            mine_b, token = band(core_arg, record, FIRST, HALF, inv, token)
            mine.append(mine_b)
            twin += [lax.ppermute(mine_b[i], "grp", swap) for i in range(HALF - FIRST)]
        if step in TURN:
            part, token = turn(mine[TURN.index(step)], token)
            turned.append(part)
        for what, g, part in sorted(todo.get(step, ()), key=lambda item: item[0] in ("pass_over", "cross")):
            first = g * GROUP
            ks = range(first, first + GROUP)
            r, begin = chunk_of(first)
            if what == "collect":
                *given, token = gather(owner_order, token, ks, held)
                kept[g] = [lax.ppermute(x, "grp", swap) for x in given]
            elif what == "select":
                near, token = gather(owner_order, token, ks, held, kept[g])
                if r:
                    near = lax.ppermute(near, "blk", [(b, (b + r) % groups) for b in range(groups)])
                nears[g] = near
            elif what == "pass_over":
                fars[g] = lax.ppermute(nears[g], "grp", swap)
            else:
                own, count = turned[begin // FIRST], GROUP // PARTS
                out, token = cross(out, token, core_arg, own, nears[g], fars[g], r, begin, part * count, count)
    return out


def solution(mesh):
    return jax.shard_map(
        body,
        mesh=mesh,
        in_specs=(P(None, ("blk", "grp")), P()),
        out_specs=P(None, None, None, ("blk", "grp"), None),
        check_vma=False,
    )
```

```python
import functools
import math

import jax
import jax.numpy as jnp
import numpy as np
from jax import lax
from jax.experimental import pallas as pl
from jax.experimental.pallas import tpu as pltpu
from jax.sharding import PartitionSpec as P

WIN = 256
NS = 128
NB = 16
BIN_LO = 8
ROUNDS = 4
HOP = 64
WG = 16
CORES = 2
HALF = NB // CORES
FIRST = 4
GROUP = 4
PICK = 3
GIVE = 5
TAIL = (2, 5, 9, 11)
PARTS, TURN = 2, (5, 7)
GAP = 5
REST_AT = 1
LAG = 2
ORDER = ((1, 0), (1, 1), (3, 0), (3, 1), (2, 0), (2, 1), (0, 0), (0, 1))
VMEM = 8 * 2**20
SHORT = pl.CostEstimate(flops=1, bytes_accessed=1, transcendentals=0)


def band_table():
    n = np.arange(NS)
    q = BIN_LO + np.arange(NB)
    phase = ((q[:, None] * n[None, :]) % NS) * (2.0 * math.pi / NS)
    taper = 0.5 - 0.5 * np.cos(n * (2.0 * math.pi / NS))
    scale = 1.0 / math.sqrt(3.0 * NS / 8.0)
    real = taper * np.cos(phase) * scale
    imag = -taper * np.sin(phase) * scale
    return np.stack([real, imag], axis=1).astype(np.float32)


def tables(lo, hi):
    table = band_table().reshape(CORES, HALF, 2, NS)[:, lo:hi].swapaxes(0, 1)
    out = np.stack([np.roll(table, w * HOP, axis=-1) for w in range(WG)], axis=-2)
    return jnp.asarray(out.reshape(-1, NS).astype(jnp.bfloat16))


def in_hbm():
    return pl.BlockSpec(memory_space=pltpu.MemorySpace.HBM)


def token_shape():
    return jax.ShapeDtypeStruct((8, 128), jnp.int32)


def in_place():
    return pl.BlockSpec(memory_space=pl.ANY)


def half_energy(x):
    wide = x.astype(jnp.float32)
    return jnp.sum((wide * wide).reshape(-1, HOP, x.shape[-1]), axis=1)


def band_kernel(first, core_ref, main_ref, halo_ref, rows_ref, *refs):
    *refs, table = refs

    @pl.when(pl.program_id(0) == 0)
    def _():
        rows = rows_ref[...].astype(jnp.float32)
        start = (lax.broadcasted_iota(jnp.int32, rows.shape, 0) & (WG - 1)) * HOP
        lane = lax.broadcasted_iota(jnp.int32, rows.shape, 1)
        for at in range(0, table.shape[1], NS):
            sample = lane + at - start
            table[:, at : at + NS] = jnp.where((sample >= 0) & (sample < NS), rows, 0.0).astype(jnp.bfloat16)

    main, halo = main_ref[...], halo_ref[...]
    if first:
        out, inv_ref, _ = refs
        energy = half_energy(main)
        later = jnp.concatenate([energy[1:], half_energy(halo)], axis=0)
        inv = 1.0 / jnp.sqrt((energy + later) / NS + 1e-05)
        inv_ref[...] = inv
    else:
        inv_ref, _, out, _ = refs
        inv = inv_ref[...]
    split = WG * HOP
    raw = jnp.dot(table[:, :split], main, preferred_element_type=jnp.float32)
    raw += jnp.dot(table[:, split : split + HOP], halo, preferred_element_type=jnp.float32)
    raw = raw.reshape(-1, CORES, 2, WG, main.shape[1])
    out[...] = (raw * inv).astype(jnp.bfloat16)


def band(core, record, lo, hi, inv=None, token=None):
    channels = record.shape[1]
    table = tables(lo, hi)
    rows, width = table.shape[0], (WG // 2 + 1) * NS
    first = inv is None
    inv_spec = pl.BlockSpec((WG, channels), lambda i: (i, 0))
    in_specs = [
        pl.BlockSpec(memory_space=pltpu.SMEM),
        pl.BlockSpec((WG * HOP, channels), lambda i: (i, 0)),
        pl.BlockSpec((HOP, channels), lambda i: ((i + 1) * WG, 0)),
        pl.BlockSpec(table.shape, lambda i: (0, 0)),
    ]
    out_specs = [pl.BlockSpec((hi - lo, CORES, 2, WG, channels), lambda i: (0, 0, 0, i, 0))]
    out_shape = [jax.ShapeDtypeStruct((hi - lo, CORES, 2, WIN, channels), jnp.bfloat16)]
    args = [core, record, record, table]
    if first:
        out_specs.append(inv_spec)
        out_shape.append(jax.ShapeDtypeStruct((WIN, channels), jnp.float32))
    else:
        in_specs += [inv_spec, in_place()]
        args += [inv, token]
    return pl.pallas_call(
        functools.partial(band_kernel, first),
        grid=(WIN // WG,),
        in_specs=in_specs,
        out_specs=out_specs + [in_place()],
        out_shape=out_shape + [token_shape()],
        scratch_shapes=[pltpu.VMEM((rows, width), jnp.bfloat16)],
        name="band_first" if first else "band_rest",
        compiler_params=pltpu.CompilerParams(vmem_limit_bytes=VMEM),
        cost_estimate=pl.CostEstimate(
            flops=2 * rows * (WIN // WG) * width * channels, bytes_accessed=3 * record.size, transcendentals=0
        ),
    )(*args)


def turn_kernel(in_ref, _, out_ref, __):
    for part in range(2):
        out_ref[0, 0, :, part * WIN : (part + 1) * WIN] = in_ref[0, 0, part].T


def turn(spectra, token):
    count, channels = spectra.shape[0], spectra.shape[-1]
    return pl.pallas_call(
        turn_kernel,
        grid=(count, CORES),
        in_specs=[pl.BlockSpec((1, 1, 2, WIN, channels), lambda i, h: (i, h, 0, 0, 0)), in_place()],
        out_specs=[pl.BlockSpec((1, 1, channels, 2 * WIN), lambda i, h: (i, h, 0, 0)), in_place()],
        out_shape=[jax.ShapeDtypeStruct((count, CORES, channels, 2 * WIN), jnp.bfloat16), token_shape()],
        name="turn",
        compiler_params=pltpu.CompilerParams(vmem_limit_bytes=VMEM),
        cost_estimate=SHORT,
    )(spectra, token)


def place(arrays, a):
    for i, b in enumerate(arrays):
        if b is a:
            return i
    arrays.append(a)
    return len(arrays) - 1


def seat():
    member = lax.axis_index("grp")
    return lax.axis_index("blk"), member // CORES, member % CORES, lax.axis_size("grp") // CORES


def chunk_of(k):
    r, half = ORDER[k // GROUP]
    return r, half * GROUP + k % GROUP


def asked_of(orders, k):
    r, _ = chunk_of(k)
    return orders[r, lax.rem(lax.axis_index("blk") + r, lax.axis_size("blk"))]


def inject(orders, token, step, mine, twin, held):
    chips = lax.axis_size("grp") // CORES
    sent = [step - LAG * hop for hop in range(chips)]
    hops = [hop for hop in range(chips) if 0 <= sent[hop] < ROUNDS * HALF]
    arrays, slots = [], {}
    for hop in hops:
        _, row = chunk_of(sent[hop])
        slots[hop] = (place(arrays, mine[row // FIRST]), row % FIRST), (place(arrays, twin[row]), None)
    whole = twin[0].shape

    def kernel(orders_ref, *refs):
        ins, out, buffer, sem = refs[: len(arrays)], refs[-4], refs[-2], refs[-1]
        _, chip, core, _ = seat()
        seen = jnp.where(core == 0, chip, chips - 1 - chip)
        for hop in hops:
            owner = asked_of(orders_ref, sent[hop])
            here = (seen == hop) & (owner // CORES == chip)
            for (slot, row), same in zip(slots[hop], (True, False), strict=True):
                source = ins[slot] if row is None else ins[slot].at[row]

                @pl.when(here & ((owner % CORES == core) == same))
                def _(source=source):
                    load = pltpu.make_async_copy(source, buffer, sem.at[0])
                    load.start()
                    load.wait()
                    store = pltpu.make_async_copy(buffer, out, sem.at[1])
                    store.start()
                    store.wait()

    in_specs = [pl.BlockSpec(memory_space=pltpu.SMEM)] + [in_hbm()] * len(arrays) + [in_place()]
    args = [orders, *arrays, token]
    aliases = {}
    if held is not None:
        in_specs.append(in_place())
        args.append(held)
        aliases = {len(args) - 1: 0}
    return pl.pallas_call(
        kernel,
        in_specs=in_specs,
        out_specs=[in_place()] * 2,
        out_shape=[jax.ShapeDtypeStruct(whole, jnp.bfloat16), token_shape()],
        input_output_aliases=aliases,
        scratch_shapes=[pltpu.VMEM(whole, jnp.bfloat16), pltpu.SemaphoreType.DMA((2,))],
        name="inject",
        compiler_params=pltpu.CompilerParams(vmem_limit_bytes=4 * 2**20),
        cost_estimate=SHORT,
    )(*args)


def gather(orders, token, ks, held, swapped=None):
    arrays = []
    chips = lax.axis_size("grp") // CORES
    slots = {(k, j): place(arrays, held[k + LAG * j]) for k in ks for j in range(chips - 1)}
    extra = [] if swapped is None else swapped
    apart = swapped is None
    shape = held[0].shape[1:]

    def kernel(orders_ref, *refs):
        ins, sems = refs[: len(arrays)], refs[-1]
        outs = refs[-2 - len(ks) : -2] if apart else [refs[-3].at[m] for m in range(len(ks))]
        _, chip, core, _ = seat()
        hop = jnp.where(core == 0, chip, chips - 1 - chip)
        home = asked_of(orders_ref, ks[0]) // CORES
        has = (hop >= 1) & ((home == chip) | ((core == 0) == (home < chip)))
        half = 1 - core if apart else core
        lead = jnp.maximum(hop, 1) - 1
        for j in range(chips - 1):

            @pl.when((lead == j) & (lead == j if apart else has))
            def _(j=j):
                for m, k in enumerate(ks):
                    pltpu.make_async_copy(ins[slots[k, j]].at[half], outs[m], sems.at[m]).start()

        if not apart:

            @pl.when(jnp.logical_not(has))
            def _():
                for m in range(len(ks)):
                    pltpu.make_async_copy(refs[len(arrays) + m], outs[m], sems.at[m]).start()

        for m in range(len(ks)):
            pltpu.make_async_copy(outs[m], outs[m], sems.at[m]).wait()

    in_vmem = pl.BlockSpec(memory_space=pltpu.VMEM)
    if apart:
        out_specs, out_shape = [in_vmem] * len(ks), [jax.ShapeDtypeStruct(shape, jnp.bfloat16)] * len(ks)
    else:
        out_specs, out_shape = [in_vmem], [jax.ShapeDtypeStruct((len(ks), *shape), jnp.bfloat16)]
    return pl.pallas_call(
        kernel,
        in_specs=[pl.BlockSpec(memory_space=pltpu.SMEM)] + [in_place()] * (len(arrays) + len(extra) + 1),
        out_specs=out_specs + [in_place()],
        out_shape=out_shape + [token_shape()],
        scratch_shapes=[pltpu.SemaphoreType.DMA((len(ks),))],
        name="collect" if apart else "select",
        compiler_params=pltpu.CompilerParams(vmem_limit_bytes=8 * 2**20),
        cost_estimate=SHORT,
    )(orders, *arrays, *extra, token)


def cross_kernel(core_ref, own_ref, near_ref, far_ref, *refs):
    out_ref = refs[-2]

    def emit(paired_ref):
        own = own_ref[0, 0]
        turned = jnp.concatenate([own[:, WIN:], -own[:, :WIN]], axis=1)
        paired = paired_ref[0].reshape(2 * WIN, -1)
        scale = 1.0 / math.sqrt(WIN)
        for part, lhs in enumerate((own, turned)):
            total = jnp.dot(lhs, paired, preferred_element_type=jnp.float32)
            out_ref[0, part, 0] = (total * scale).astype(jnp.bfloat16)

    @pl.when(pl.program_id(0) == 0)
    def _():
        emit(near_ref)

    @pl.when(pl.program_id(0) == 1)
    def _():
        emit(far_ref)


def cross(out, token, core, own, near, far, round_index, first_chunk, begin, count):
    channels = near.shape[-1]
    first_chunk += begin
    row = first_chunk % own.shape[0]
    block = (1, 2, WIN, channels)
    near_spec = pl.BlockSpec(block, lambda g, i, c: (begin + jnp.where(g == 0, i, count - 1), 0, 0, 0))
    far_spec = pl.BlockSpec(block, lambda g, i, c: (begin + jnp.where(g == 0, 0, i), 0, 0, 0))
    in_specs = [
        pl.BlockSpec((1, 1, channels, 2 * WIN), lambda g, i, c: (row + i, (c[0] + g) % CORES, 0, 0)),
        near_spec,
        far_spec,
        in_place(),
    ]
    out_spec = pl.BlockSpec(
        (1, 2, 1, channels, channels),
        lambda g, i, c: (round_index, 0, ((c[0] + g) % CORES) * HALF + first_chunk + i, 0, 0),
    )
    args = [core, own, near, far, token]
    aliases = {}
    if out is not None:
        in_specs.append(in_place())
        args.append(out)
        aliases = {len(args) - 1: 0}
    return pl.pallas_call(
        cross_kernel,
        grid_spec=pltpu.PrefetchScalarGridSpec(
            num_scalar_prefetch=1, grid=(CORES, count), in_specs=in_specs, out_specs=[out_spec, in_place()]
        ),
        out_shape=[jax.ShapeDtypeStruct((ROUNDS, 2, NB, channels, channels), jnp.bfloat16), token_shape()],
        input_output_aliases=aliases,
        name="cross",
        compiler_params=pltpu.CompilerParams(vmem_limit_bytes=VMEM),
        cost_estimate=SHORT,
    )(*args)


def body(record, owner_order):
    groups, members = lax.axis_size("blk"), lax.axis_size("grp")
    chips = members // CORES
    core_arg = (lax.axis_index("grp") % CORES).reshape(1).astype(jnp.int32)

    flow = [(m, m + CORES) for m in range(0, members - CORES, CORES)]
    flow += [(m + CORES, m) for m in range(1, members - CORES, CORES)]
    swap = [(m, m ^ 1) for m in range(members)]
    chunks = ROUNDS * HALF
    steps = chunks + LAG * (chips - 2)

    mine_a, inv, token = band(core_arg, record, 0, FIRST)
    mine, twin = [mine_a], [lax.ppermute(mine_a[i], "grp", swap) for i in range(FIRST)]

    arrived, held, turned = [], [], []
    out = None
    kept, nears, fars = {}, {}, {}
    todo = {}
    for g in range(chunks // GROUP):
        at = (g + 1) * GROUP - 1 + LAG * (chips - 2) + LAG
        across = bool(ORDER[g][0])
        left = chunks // GROUP - 1 - g
        pick = at + (1 if left == 0 else PICK)
        give = pick + GIVE if across else pick
        meet = at + TAIL[left] if left < 4 else give + GAP
        plan = ((at, "collect", 0), (pick, "select", 0), (give, "pass_over", 0), *((meet + i * (left >= 4), "cross", i) for i in range(PARTS if left >= 4 else 1)))
        for wait, what, part in plan:
            todo.setdefault(wait, []).append((what, g, part))

    for step in range(max(todo) + 1):
        if step < steps + LAG:
            buffer = arrived[step - LAG] if step >= LAG else None
            sent, token = inject(owner_order, token, step, mine, twin, buffer)
            if step < steps:
                arrived.append(lax.ppermute(sent, "grp", flow))
            if step >= LAG:
                held.append(sent)
        if step == REST_AT:
            mine_b, token = band(core_arg, record, FIRST, HALF, inv, token)
            mine.append(mine_b)
            twin += [lax.ppermute(mine_b[i], "grp", swap) for i in range(HALF - FIRST)]
        if step in TURN:
            part, token = turn(mine[TURN.index(step)], token)
            turned.append(part)
        for what, g, part in sorted(todo.get(step, ()), key=lambda item: item[0] in ("pass_over", "cross")):
            first = g * GROUP
            ks = range(first, first + GROUP)
            r, begin = chunk_of(first)
            if what == "collect":
                *given, token = gather(owner_order, token, ks, held)
                kept[g] = [lax.ppermute(x, "grp", swap) for x in given]
            elif what == "select":
                near, token = gather(owner_order, token, ks, held, kept[g])
                if r:
                    near = lax.ppermute(near, "blk", [(b, (b + r) % groups) for b in range(groups)])
                nears[g] = near
            elif what == "pass_over":
                fars[g] = lax.ppermute(nears[g], "grp", swap)
            else:
                own, count = turned[begin // FIRST], GROUP // (PARTS if g < chunks // GROUP - 4 else 1)
                out, token = cross(out, token, core_arg, own, nears[g], fars[g], r, begin, part * count, count)
    return out


def solution(mesh):
    return jax.shard_map(
        body,
        mesh=mesh,
        in_specs=(P(None, ("blk", "grp")), P()),
        out_specs=P(None, None, None, ("blk", "grp"), None),
        check_vma=False,
    )
```
